32 devices in a mesh: groups: 2 (over y), row: 4 (over x, core), col: 4 (over z).
Axes of the slice: x: 2, y: 2, z: 4, core: 2. Of those that a mesh axis runs over, the one named last changes fastest.
Arguments:
- slope_matrix: bfloat16 [1024, 1024], P(('groups', 'row'), 'col'), parts along dimension 0, may hold values from -0.3125 to 0.3125
- prior_matrix: bfloat16 [1024, 1024], P(('groups', 'row'), 'col'), parts along dimension 0, may hold values from -0.3125 to 0.3125
- slope_blocks: int32 [8, 8], P(('groups', 'row'), 'col'), parts along dimension 0, may hold values from 0 to 23, as said below
- prior_blocks: int32 [8, 8], P(('groups', 'row'), 'col'), parts along dimension 0, may hold values from 0 to 23, as said below
- weight_ids: int32 [512], P(('groups', 'row')), parts along dimension 0, may hold values from 0 to 15
- valid_mask: int32 [512], P(('groups', 'row')), parts along dimension 0, may hold values 0 or 1
- noise_weights: float32 [32], P('groups'), parts along dimension 0, may hold values from 0.25 to 4
- prior_weights: bfloat16 [1024], P(('groups', 'row')), parts along dimension 0, may hold values from 0.19921875 to 2
- frames: float32 [6144, 64], P(('groups', 'row', 'col')), parts along dimension 0, may hold values from -6 to 6
Outputs:
- gram_matrix: float32 [6144, 3072], P(('groups', 'row'), 'col'), parts along dimension 0
- applied: float32 [6144, 64], P(('groups', 'row', 'col')), parts along dimension 0
The draws below stay inside these ranges and needn't reach their ends.
There are 2 independent parts, one for each index of `groups`. The reference program is written for one: setup_inputs(seed, part) draws one part's arguments, and reference() takes and returns one part's arrays. A program takes and returns all parts, laid end to end along the dimension named above; each array names one. Nothing has to cross between parts.
Inputs may be any that keep to these rules, and one draw needn't show every extreme that they name: `slope_blocks`: row i names, for each block-column set c (entries c * 2 to c * 2 + 1), 2 distinct actuator blocks of that set, c * 6 to c * 6 + 5, in the order in which their blocks are stored. `prior_blocks`: row i names, for each block-column set c (entries c * 2 to c * 2 + 1), 2 distinct actuator blocks of that set, c * 6 to c * 6 + 5, in the order in which their blocks are stored.
All inputs are finite; a program needn't handle non-finite values. No bound on the sum of `valid_mask` on one device may be relied on, other than what follows from the above.
Results may differ from the reference program's by a relative error of at most 0.007.
Values may be sent and summed in bfloat16 or wider, within the bound.
A program may use at most 128 MiB of HBM per device.

```python
import math
import jax
import jax.numpy as jnp
from jax import lax

BS = 128
AB = 6
KD = 2
SB = 1
PB = 1
F = 64
NW = 16
NA = 24
NS = 512
NP = 512
NSUB = 256
N_ROW = 4
N_COL = 4


def draw_blocks(key, block_rows):
    scores = jax.random.randint(key, (block_rows, N_COL, AB), 1, 1 << 20)
    local = jnp.arange(AB, dtype=jnp.int32)
    first_row = (jnp.arange(block_rows, dtype=jnp.int32) == 0)[:, None, None]
    end_blocks = ((local == 0) | (local == AB - 1))[None, None, :]
    scores = jnp.where(first_row & end_blocks, 0, scores)
    keyed = scores * AB + local[None, None, :]
    ordering = jnp.argsort(keyed, axis=2)
    chosen = ordering[:, :, :KD].astype(jnp.int32)
    set_start = jnp.arange(N_COL, dtype=jnp.int32)[None, :, None] * AB
    return (chosen + set_start).reshape(block_rows, N_COL * KD)


def draw_slope_blocks(key, part):
    return draw_blocks(jax.random.fold_in(key, 3), SB * N_ROW)


def draw_prior_blocks(key, part):
    return draw_blocks(jax.random.fold_in(key, 7), PB * N_ROW)


def touch_ends(result, own_key, smallest, high):
    shape = result.shape
    place = [jax.random.randint(jax.random.fold_in(own_key, axis), (), 0, shape[axis]) for axis in range(len(shape))]
    result = result.at[tuple(place)].set(smallest)
    longest = shape.index(max(shape))
    place[longest] = (place[longest] + 1) % shape[longest]
    return result.at[tuple(place)].set(high)


def shard_levels(own_key, dims, shards, smallest, largest):
    loudness, own = 1.0, jax.random.fold_in(own_key, 6)
    for dim, shards_of in shards:
        draws = jnp.exp(jax.random.uniform(jax.random.fold_in(own, dim), (shards_of,), jnp.float32, smallest / len(shards), largest / len(shards)))
        loudness = loudness * jnp.repeat(draws, dims[dim] // shards_of).reshape([-1 if axis == dim else 1 for axis in range(len(dims))])
    return loudness


def bell_draw(key, shape, spread, bound, shards=(), kind=jnp.bfloat16):
    array = jax.random.normal(key, shape, jnp.float32) * spread
    if len(shards) > 0:
        array = shard_levels(key, shape, shards, -0.22, 0.18) * array
    return jnp.clip(array, min=-bound, max=bound).astype(kind)


def setup_inputs(seed: int = 0, part: int = 0) -> dict:
    key_of = jax.random.split(jax.random.key(seed), 10)
    part_splits = jax.random.split(jax.random.fold_in(key_of[9], part), 10)
    slope_matrix = bell_draw(part_splits[0], (NS, N_COL * KD * BS), (N_ROW * (SB + PB) * BS * KD // AB) ** -0.5, 0.3125, ((0, 4), (1, 4)))
    prior_matrix = bell_draw(part_splits[1], (NP, N_COL * KD * BS), (N_ROW * (SB + PB) * BS * KD // AB) ** -0.5, 0.3125, ((0, 4), (1, 4)))
    slope_blocks = draw_slope_blocks(jax.random.fold_in(jax.random.fold_in(key_of[9], part), 71), part)
    prior_blocks = draw_prior_blocks(jax.random.fold_in(jax.random.fold_in(key_of[9], part), 71), part)
    weight_ids = touch_ends(jax.random.randint(part_splits[4], (NSUB,), 0, NW), jax.random.fold_in(part_splits[4], 1), 0, NW - 1).astype(jnp.int32)
    valid_mask = touch_ends((jax.random.randint(part_splits[5], (NSUB,), 0, 4) < 3).astype(jnp.int32), jax.random.fold_in(part_splits[5], 1), 0, 1)
    noise_weights = jnp.clip(jnp.exp(jax.random.uniform(part_splits[6], (NW,), jnp.float32, math.log(0.25), math.log(4.0))), 0.25, 4.0)
    prior_weights = jnp.clip(jnp.exp(math.log(2.0) - 2.306499 * jax.random.uniform(part_splits[7], (NP,), jnp.float32) ** shard_levels(part_splits[7], (NP,), ((0, 4),), -0.2, 0.2)), 0.19921875, 2.0).astype(jnp.bfloat16)
    frames = bell_draw(part_splits[8], (NA * BS, F), 1.0, 6.0, ((0, 16),), jnp.float32)
    return dict(slope_matrix=slope_matrix, prior_matrix=prior_matrix, slope_blocks=slope_blocks, prior_blocks=prior_blocks, weight_ids=weight_ids, valid_mask=valid_mask, noise_weights=noise_weights, prior_weights=prior_weights, frames=frames)


def expand_all(values, block_ids):
    block_count = block_ids.shape[0]
    chosen = block_ids.shape[1]
    targets = jnp.arange(NA, dtype=jnp.int32)
    onehot = (block_ids[:, :, None] == targets[None, None, :]).astype(jnp.float32)
    shaped = values.astype(jnp.float32).reshape(block_count, BS, chosen, BS)
    expanded = jnp.einsum("rskb,rka->rsab", shaped, onehot)
    return expanded.reshape(block_count * BS, NA * BS).astype(jnp.bfloat16)


def reference(slope_matrix, prior_matrix, slope_blocks, prior_blocks, weight_ids, valid_mask, noise_weights, prior_weights, frames):
    subap_weight = noise_weights[weight_ids] * valid_mask.astype(jnp.float32)
    slope_weight = jnp.repeat(subap_weight, 2).astype(jnp.bfloat16)
    slope_dense = expand_all(slope_matrix, slope_blocks)
    prior_dense = expand_all(prior_matrix, prior_blocks)
    slope_weighted = (slope_dense.astype(jnp.float32) * slope_weight.astype(jnp.float32)[:, None]).astype(jnp.bfloat16)
    prior_weighted = (prior_dense.astype(jnp.float32) * prior_weights.astype(jnp.float32)[:, None]).astype(jnp.bfloat16)
    slope_part = jnp.dot(slope_dense.astype(jnp.float32).T, slope_weighted.astype(jnp.float32), preferred_element_type=jnp.float32)
    prior_part = jnp.dot(prior_dense.astype(jnp.float32).T, prior_weighted.astype(jnp.float32), preferred_element_type=jnp.float32)
    gram_matrix = slope_part + prior_part
    applied = jnp.dot(gram_matrix, frames, precision=lax.Precision.HIGHEST, preferred_element_type=jnp.float32)
    return (gram_matrix, applied)
```

```python
import functools

import jax
import jax.numpy as jnp
from jax import lax
from jax.experimental import pallas as pl
from jax.experimental.pallas import tpu as pltpu
from jax.sharding import PartitionSpec as P

BS = 128
AB = 6
EXTRA = 16
MESH = pl.DeviceIdType.MESH


def remote(src, dst, send, recv, axis, to):
    return pltpu.make_async_remote_copy(
        src_ref=src, dst_ref=dst, send_sem=send, recv_sem=recv,
        device_id={axis: to}, device_id_type=MESH,
    )


def exchange(
    n, ids_ref, slope_ref, prior_ref, extra_ref, frames_ref,
    blocks, images,
    held, own_frames, set_frames, partial,
    send_z, recv_z, send_c, recv_c, send_r, recv_r,
    send_p, recv_p, send_f, recv_f, send_v, recv_v, send_u, recv_u,
):
    row = lax.axis_index("row")
    col = lax.axis_index("col")
    rows = slope_ref.shape[0]
    piece = own_frames.shape[0]
    barrier = pltpu.get_barrier_semaphore()
    for t in range(1, n):
        pl.semaphore_signal(barrier, inc=1, device_id={"col": lax.rem(col + t, n)}, device_id_type=MESH)
        pl.semaphore_signal(barrier, inc=1, device_id={"row": lax.rem(row + t, n)}, device_id_type=MESH)
    own_frames[...] = frames_ref[...].astype(jnp.bfloat16)
    held[col, pl.ds(0, rows), :] = slope_ref[...]
    held[col, pl.ds(rows, rows), :] = prior_ref[...]
    held[col, pl.ds(2 * rows, EXTRA), :] = extra_ref[...]
    pl.semaphore_wait(barrier, 2 * (n - 1))

    def frame_piece(source):
        return remote(
            own_frames, set_frames.at[pl.ds(source * piece, piece), :],
            send_p, recv_p.at[source], "col", row,
        )

    @pl.when(row != col)
    def _():
        frame_piece(col).start()

    sends_z = []
    for t in range(1, n):
        copy = remote(
            held.at[col], held.at[col], send_z.at[t - 1], recv_z.at[t - 1], "col", lax.rem(col + t, n)
        )
        copy.start()
        sends_z.append(copy)
    sends_c = []
    for s in range(1, n):
        copy = remote(
            held.at[col], blocks.at[0, row], send_c.at[s - 1], recv_c.at[s - 1], "row", lax.rem(row + s, n)
        )
        copy.start()
        sends_c.append(copy)
    blocks[0, row] = held[col]

    def whole_frames(s):
        return remote(
            set_frames, set_frames, send_f.at[s - 1], recv_f, "row", lax.rem(row + s, n)
        )

    @pl.when(row == col)
    def _():
        set_frames[pl.ds(col * piece, piece), :] = own_frames[...]
        for t in range(1, n):
            frame_piece(lax.rem(col + t, n)).wait_recv()
        for s in range(1, n):
            whole_frames(s).start()

    @pl.when(row != col)
    def _():
        whole_frames(1).wait_recv()

    parts = []
    for part, ref in enumerate((slope_ref, prior_ref)):
        total = jnp.zeros((rows, set_frames.shape[1]), jnp.float32)
        for k in range(ref.shape[1] // BS):
            wanted = jnp.full((BS, set_frames.shape[1]), ids_ref[part * (ref.shape[1] // BS) + k], jnp.int32)
            chosen = jnp.zeros(wanted.shape, jnp.float32)
            for a in range(AB):
                block = set_frames[a * BS:(a + 1) * BS, :].astype(jnp.float32)
                chosen = jnp.where(wanted == a, block, chosen)
            total += jnp.dot(
                ref[:, k * BS:(k + 1) * BS], chosen.astype(jnp.bfloat16),
                preferred_element_type=jnp.float32,
            )
        parts.append(total)
    partial[col] = jnp.concatenate(parts, axis=1).astype(jnp.bfloat16)
    sends_v = []
    for t in range(1, n):
        copy = remote(
            partial.at[col], partial.at[col], send_v.at[t - 1], recv_v.at[t - 1], "col", lax.rem(col + t, n)
        )
        copy.start()
        sends_v.append(copy)

    def forward(t):
        source = lax.rem(col + n - t, n)
        return remote(
            held.at[source], blocks.at[1, row], send_r.at[t - 1],
            recv_r.at[lax.rem(source + n - row, n)], "row", source,
        )

    for t in range(1, n):
        sends_z[t - 1].wait_recv()
        source = lax.rem(col + n - t, n)

        @pl.when(source == row)
        def _():
            blocks[1, row] = held[row]

        @pl.when(source != row)
        def _():
            forward(t).start()

    for copy in sends_v:
        copy.wait_recv()
    image = partial[0].astype(jnp.float32)
    for t in range(1, n):
        image += partial[t].astype(jnp.float32)
    images[row] = image.astype(jnp.bfloat16)
    sends_u = []
    for s in range(1, n):
        copy = remote(
            images.at[row], images.at[row], send_u.at[s - 1], recv_u.at[s - 1], "row", lax.rem(row + s, n)
        )
        copy.start()
        sends_u.append(copy)

    for copy in sends_c:
        copy.wait_recv()

    @pl.when(row != col)
    def _():
        for s in range(1, n):
            source = lax.rem(row + n - s, n)
            remote(
                held.at[0], blocks.at[1, source], send_r.at[0], recv_r.at[s], "row", source
            ).wait_recv()
        frame_piece(col).wait_send()

    @pl.when(row == col)
    def _():
        for s in range(1, n):
            whole_frames(s).wait_send()

    for copy in sends_u:
        copy.wait_recv()
    for t in range(1, n):

        @pl.when(lax.rem(col + n - t, n) != row)
        def _():
            forward(t).wait_send()

    for copy in sends_z + sends_c + sends_v + sends_u:
        copy.wait_send()


def combine(n, ids_ref, blocks, images, gram, applied, total):
    rows = images.shape[1]
    kept = blocks.shape[3] // BS
    wide = images.shape[2] // 2
    same = ids_ref[4 * n * kept]
    quarter = ids_ref[4 * n * kept + 1]
    gram[...] = jnp.zeros_like(gram)
    total[...] = jnp.zeros_like(total)
    for i in range(n):
        for part in range(2):
            left = blocks[same, i, part * rows:(part + 1) * rows, :]
            right = blocks[0, i, part * rows:(part + 1) * rows, :].astype(jnp.float32)
            weight = blocks[0, i, 2 * rows:2 * rows + EXTRA, part * rows:(part + 1) * rows]
            weight = weight.astype(jnp.float32)[1:2, :]
            weight = jnp.transpose(jnp.broadcast_to(weight, (BS, rows)))
            right = jnp.concatenate(
                [right[:, k * BS:(k + 1) * BS] * weight for k in range(kept)], axis=1
            ).astype(jnp.bfloat16)
            image = images[i, :, part * wide:(part + 1) * wide].astype(jnp.float32)
            image = (image * weight[:, :wide]).astype(jnp.bfloat16)
            over = (((0,), (0,)), ((), ()))
            product = lax.dot_general(left, right, over, preferred_element_type=jnp.float32)
            shown = lax.dot_general(left, image, over, preferred_element_type=jnp.float32)
            for a in range(kept):
                down = ids_ref[(same * n + i) * 2 * kept + part * kept + a]
                down = pl.multiple_of(down * BS, BS)
                total[pl.ds(down, BS), :] += shown[a * BS:(a + 1) * BS]
                for b in range(kept):
                    across = ids_ref[i * 2 * kept + part * kept + b]
                    across = pl.multiple_of(across * BS, BS)
                    gram[pl.ds(down, BS), pl.ds(across, BS)] += product[
                        a * BS:(a + 1) * BS, b * BS:(b + 1) * BS
                    ]
    size = applied.shape[0]
    applied[...] = total[pl.ds(pl.multiple_of(quarter * size, 8), size), :]


def shards(
    n, slope_matrix, prior_matrix, slope_blocks, prior_blocks,
    weight_ids, valid_mask, noise_weights, prior_weights, frames,
):
    row = lax.axis_index("row")
    col = lax.axis_index("col")
    rows, width = slope_matrix.shape
    kept = width // BS
    piece, wide = frames.shape
    classes = jnp.arange(noise_weights.shape[0], dtype=jnp.int32)
    picked = jnp.sum(
        jnp.where(weight_ids[:, None] == classes[None, :], noise_weights[None, :], 0.0), axis=1
    )
    subap_weight = picked * valid_mask.astype(jnp.float32)
    slope_weight = jnp.repeat(subap_weight, 2).astype(jnp.bfloat16)
    ids = jnp.concatenate([slope_blocks[0], prior_blocks[0]]) - col * AB
    weight = jnp.concatenate([slope_weight, prior_weights])
    extra = jnp.concatenate(
        [
            jnp.pad(ids.astype(jnp.bfloat16), (0, width - 2 * kept))[None],
            weight[None],
            jnp.zeros((EXTRA - 2, width), jnp.bfloat16),
        ]
    )
    vmem = pl.BlockSpec(memory_space=pltpu.VMEM)
    smem = pl.BlockSpec(memory_space=pltpu.SMEM)
    tall = 2 * rows + EXTRA
    pairs = pltpu.SemaphoreType.DMA((n,))
    blocks, images = pl.pallas_call(
        functools.partial(exchange, n),
        out_shape=(
            jax.ShapeDtypeStruct((2, n, tall, width), jnp.bfloat16),
            jax.ShapeDtypeStruct((n, rows, 2 * wide), jnp.bfloat16),
        ),
        in_specs=[smem] + [vmem] * 4,
        out_specs=(vmem, vmem),
        scratch_shapes=[
            pltpu.VMEM((n, tall, width), jnp.bfloat16),
            pltpu.VMEM((piece, wide), jnp.bfloat16),
            pltpu.VMEM((n * piece, wide), jnp.bfloat16),
            pltpu.VMEM((n, rows, 2 * wide), jnp.bfloat16),
            pairs, pairs, pairs, pairs, pairs, pairs,
            pltpu.SemaphoreType.DMA, pairs,
            pairs, pltpu.SemaphoreType.DMA,
            pairs, pairs, pairs, pairs,
        ],
        compiler_params=pltpu.CompilerParams(
            collective_id=0, has_side_effects=True, vmem_limit_bytes=32 * 1024 * 1024
        ),
    )(ids, slope_matrix, prior_matrix, extra, frames)
    all_ids = blocks[:, :, 2 * rows, :2 * kept].astype(jnp.float32).astype(jnp.int32).reshape(-1)
    same = jnp.where(row == col, 0, 1).astype(jnp.int32)
    all_ids = jnp.concatenate([all_ids, same[None], col[None].astype(jnp.int32)])
    gram, applied = pl.pallas_call(
        functools.partial(combine, n),
        out_shape=(
            jax.ShapeDtypeStruct((AB * BS, AB * BS), jnp.float32),
            jax.ShapeDtypeStruct((piece, wide), jnp.float32),
        ),
        in_specs=[smem, vmem, vmem],
        out_specs=(vmem, vmem),
        scratch_shapes=[pltpu.VMEM((AB * BS, wide), jnp.float32)],
        compiler_params=pltpu.CompilerParams(vmem_limit_bytes=32 * 1024 * 1024),
    )(all_ids, blocks, images)
    return gram, applied


def solution(mesh):
    in_specs = (
        P(("groups", "row"), "col"),
        P(("groups", "row"), "col"),
        P(("groups", "row"), "col"),
        P(("groups", "row"), "col"),
        P(("groups", "row")),
        P(("groups", "row")),
        P("groups"),
        P(("groups", "row")),
        P(("groups", "row", "col"), None),
    )
    out_specs = (P(("groups", "row"), "col"), P(("groups", "row", "col"), None))
    return jax.shard_map(
        functools.partial(shards, mesh.shape["row"]),
        mesh=mesh, in_specs=in_specs, out_specs=out_specs, check_vma=False,
    )
```

```python
import functools

import jax
import jax.numpy as jnp
from jax import lax
from jax.experimental import pallas as pl
from jax.experimental.pallas import tpu as pltpu
from jax.sharding import PartitionSpec as P

BS = 128
AB = 6
EXTRA = 16
MESH = pl.DeviceIdType.MESH


def remote(src, dst, send, recv, axis, to):
    return pltpu.make_async_remote_copy(
        src_ref=src, dst_ref=dst, send_sem=send, recv_sem=recv,
        device_id={axis: to}, device_id_type=MESH,
    )


def exchange(
    n, classes, slope_hbm, prior_hbm, slope_ids_hbm, prior_ids_hbm,
    class_hbm, valid_hbm, noise_hbm, prior_weight_hbm, frames_hbm,
    blocks, images,
    held, own_frames, set_frames, partial,
    slope_ids, prior_ids, class_ids, valid, noise, prior_weight, frames_ref, load_sem,
    send_right, send_left, recv_z, send_c, recv_c, send_r, recv_r,
    send_p, recv_p, send_f, recv_f, send_v, recv_v, send_u, recv_u,
):
    row = lax.axis_index("row")
    col = lax.axis_index("col")
    rows, width = slope_hbm.shape
    kept = width // BS
    piece = own_frames.shape[0]
    loads = [
        pltpu.make_async_copy(src, dst, load_sem.at[k])
        for k, (src, dst) in enumerate(
            (
                (class_hbm, class_ids), (valid_hbm, valid), (noise_hbm, noise),
                (prior_weight_hbm, prior_weight), (slope_ids_hbm, slope_ids),
                (prior_ids_hbm, prior_ids), (frames_hbm, frames_ref),
                (slope_hbm, held.at[col, pl.ds(0, rows), :]),
                (prior_hbm, held.at[col, pl.ds(rows, rows), :]),
            )
        )
    ]
    for load in loads:
        load.start()
    barrier = pltpu.get_barrier_semaphore()
    for t in range(1, n):
        pl.semaphore_signal(barrier, inc=1, device_id={"col": lax.rem(col + t, n)}, device_id_type=MESH)
        pl.semaphore_signal(barrier, inc=1, device_id={"row": lax.rem(row + t, n)}, device_id_type=MESH)
    for load in loads:
        load.wait()
    own_frames[...] = jnp.transpose(frames_ref[...]).astype(jnp.bfloat16)
    subaps = class_ids.shape[1]
    picked = jnp.zeros((1, subaps), jnp.float32)
    for k in range(classes):
        picked = jnp.where(class_ids[...] == k, jnp.broadcast_to(noise[:, k:k + 1], picked.shape), picked)
    picked = (picked * valid[...].astype(jnp.float32)).astype(jnp.bfloat16)
    first = lax.broadcasted_iota(jnp.int32, (subaps, rows), 0) * (rows // subaps)
    lane = lax.broadcasted_iota(jnp.int32, (subaps, rows), 1)
    spread = (lane >= first) & (lane < first + rows // subaps)
    spread = jnp.where(spread, 1.0, 0.0).astype(jnp.bfloat16)
    slope_weight = jnp.dot(
        jnp.broadcast_to(picked, (EXTRA, subaps)), spread, preferred_element_type=jnp.float32
    )
    prior_wide = jnp.broadcast_to(prior_weight[...].astype(jnp.float32), (EXTRA, rows))
    weight = jnp.concatenate([slope_weight, prior_wide], axis=1)
    at_row = lax.broadcasted_iota(jnp.int32, (EXTRA, width), 0)
    at_lane = lax.broadcasted_iota(jnp.int32, (EXTRA, width), 1)
    names = jnp.zeros((EXTRA, width), jnp.int32)
    for part, ids in enumerate((slope_ids, prior_ids)):
        for k in range(kept):
            name = jnp.broadcast_to(ids[:, k:k + 1], names.shape) - col * AB
            names = jnp.where(at_lane == part * kept + k, name, names)
    extra = jnp.where(at_row == 0, names.astype(jnp.float32), weight)
    held[col, pl.ds(2 * rows, EXTRA), :] = extra.astype(jnp.bfloat16)
    pl.semaphore_wait(barrier, 2 * (n - 1))

    def frame_piece(source):
        return remote(
            own_frames, set_frames.at[pl.ds(source * piece, piece), :],
            send_p, recv_p.at[source], "col", row,
        )

    def right(t):
        source = col - t
        return remote(
            held.at[source], held.at[source], send_right.at[t], recv_z.at[source], "col", col + 1
        )

    def left(t):
        source = col + t
        return remote(
            held.at[source], held.at[source], send_left.at[t], recv_z.at[source], "col", col - 1
        )

    sibling = row + 1 - 2 * lax.rem(row, 2)

    def own_column(m):
        to = sibling if m == 0 else lax.rem(row + 2 * m, n)
        return remote(held.at[col], blocks.at[0, row], send_c.at[m], recv_c.at[row], "row", to)

    def pass_column(m):
        source = lax.rem(row + 2 * m, n)
        return remote(
            blocks.at[0, source], blocks.at[0, source], send_c.at[n // 2 + m], recv_c.at[source], "row", sibling
        )

    def came_column(source):
        return remote(blocks.at[0, source], blocks.at[0, source], send_c.at[0], recv_c.at[source], "row", sibling)

    def forward(source):
        return remote(
            held.at[source], blocks.at[1, row], send_r.at[source], recv_r.at[row], "row", source
        )

    def came_row(source):
        return remote(
            held.at[source], blocks.at[1, source], send_r.at[source], recv_r.at[source], "row", source
        )

    def whole_frames(s):
        return remote(
            set_frames, set_frames, send_f.at[s - 1], recv_f, "row", lax.rem(row + s, n)
        )

    @pl.when(row != col)
    def _():
        frame_piece(col).start()

    @pl.when(col < n - 1)
    def _():
        right(0).start()

    @pl.when(col > 0)
    def _():
        left(0).start()

    for m in range(1, n // 2):
        own_column(m).start()
    own_column(0).start()
    blocks[0, row] = held[col]

    @pl.when(row == col)
    def _():
        set_frames[pl.ds(pl.multiple_of(col * piece, 16), piece), :] = own_frames[...]
        for t in range(1, n):
            frame_piece(lax.rem(col + t, n)).wait_recv()
        for s in range(1, n):
            whole_frames(s).start()

    @pl.when(row != col)
    def _():
        whole_frames(1).wait_recv()

    parts = []
    for part, ids in enumerate((slope_ids, prior_ids)):
        total = jnp.zeros((rows, set_frames.shape[1]), jnp.float32)
        for k in range(kept):
            wanted = jnp.broadcast_to(ids[:, k:k + 1], (BS, set_frames.shape[1])) - col * AB
            chosen = jnp.zeros(wanted.shape, jnp.float32)
            for a in range(AB):
                block = set_frames[a * BS:(a + 1) * BS, :].astype(jnp.float32)
                chosen = jnp.where(wanted == a, block, chosen)
            total += jnp.dot(
                held[col, part * rows:(part + 1) * rows, k * BS:(k + 1) * BS], chosen.astype(jnp.bfloat16),
                preferred_element_type=jnp.float32,
            )
        parts.append(total)
    partial[col] = jnp.concatenate(parts, axis=1).astype(jnp.bfloat16)
    sends_v = []
    for t in range(1, n):
        copy = remote(
            partial.at[col], partial.at[col], send_v.at[t - 1], recv_v.at[t - 1], "col", lax.rem(col + t, n)
        )
        copy.start()
        sends_v.append(copy)

    def use(source):
        @pl.when(source == row)
        def _():
            blocks[1, row] = held[row]

        @pl.when(source != row)
        def _():
            forward(source).start()

    for t in range(1, n):
        @pl.when(col - t >= 0)
        def _():
            came = right(t)
            came.wait_recv()

            @pl.when(col < n - 1)
            def _():
                came.start()

            use(col - t)

        @pl.when(col + t < n)
        def _():
            came = left(t)
            came.wait_recv()

            @pl.when(col > 0)
            def _():
                came.start()

            use(col + t)

        if t < n // 2:
            came_column(lax.rem(row + 2 * t, n)).wait_recv()
            pass_column(t).start()

    for copy in sends_v:
        copy.wait_recv()
    image = partial[0].astype(jnp.float32)
    for t in range(1, n):
        image += partial[t].astype(jnp.float32)
    images[row] = image.astype(jnp.bfloat16)
    sends_u = []
    for s in range(1, n):
        copy = remote(
            images.at[row], images.at[row], send_u.at[s - 1], recv_u.at[s - 1], "row", lax.rem(row + s, n)
        )
        copy.start()
        sends_u.append(copy)

    for m in range(n // 2):
        came_column(lax.rem(sibling + 2 * m, n)).wait_recv()

    @pl.when(row != col)
    def _():
        for s in range(1, n):
            came_row(lax.rem(row + s, n)).wait_recv()
        frame_piece(col).wait_send()

    @pl.when(row == col)
    def _():
        for s in range(1, n):
            whole_frames(s).wait_send()

    for copy in sends_u:
        copy.wait_recv()
    for t in range(1, n):
        source = lax.rem(col + t, n)

        @pl.when(source != row)
        def _():
            forward(source).wait_send()

    for t in range(n):
        @pl.when((col - t >= 0) & (col < n - 1))
        def _():
            right(t).wait_send()

        @pl.when((col + t < n) & (col > 0))
        def _():
            left(t).wait_send()

    for m in range(n // 2):
        own_column(m).wait_send()
        if m > 0:
            pass_column(m).wait_send()
    for copy in sends_v + sends_u:
        copy.wait_send()


def combine(n, ids_ref, blocks, images, gram, applied, total):
    rows = images.shape[1]
    kept = blocks.shape[3] // BS
    wide = images.shape[2] // 2
    same = ids_ref[4 * n * kept]
    quarter = ids_ref[4 * n * kept + 1]
    gram[...] = jnp.zeros_like(gram)
    total[...] = jnp.zeros_like(total)
    for i in range(n):
        for part in range(2):
            left = blocks[same, i, part * rows:(part + 1) * rows, :]
            right = blocks[0, i, part * rows:(part + 1) * rows, :].astype(jnp.float32)
            weight = blocks[0, i, 2 * rows:2 * rows + EXTRA, part * rows:(part + 1) * rows]
            weight = weight.astype(jnp.float32)[1:2, :]
            weight = jnp.transpose(jnp.broadcast_to(weight, (BS, rows)))
            right = jnp.concatenate(
                [right[:, k * BS:(k + 1) * BS] * weight for k in range(kept)], axis=1
            ).astype(jnp.bfloat16)
            image = images[i, :, part * wide:(part + 1) * wide].astype(jnp.float32)
            image = (image * weight[:, :wide]).astype(jnp.bfloat16)
            over = (((0,), (0,)), ((), ()))
            product = lax.dot_general(left, right, over, preferred_element_type=jnp.float32)
            shown = lax.dot_general(left, image, over, preferred_element_type=jnp.float32)
            for a in range(kept):
                down = ids_ref[(same * n + i) * 2 * kept + part * kept + a]
                down = pl.multiple_of(down * BS, BS)
                total[pl.ds(down, BS), :] += shown[a * BS:(a + 1) * BS]
                for b in range(kept):
                    across = ids_ref[i * 2 * kept + part * kept + b]
                    across = pl.multiple_of(across * BS, BS)
                    gram[pl.ds(down, BS), pl.ds(across, BS)] += product[
                        a * BS:(a + 1) * BS, b * BS:(b + 1) * BS
                    ]
    size = applied.shape[1]
    applied[...] = jnp.transpose(total[pl.ds(pl.multiple_of(quarter * size, 8), size), :])


def shards(
    n, slope_matrix, prior_matrix, slope_blocks, prior_blocks,
    weight_ids, valid_mask, noise_weights, prior_weights, frames,
):
    row = lax.axis_index("row")
    col = lax.axis_index("col")
    rows, width = slope_matrix.shape
    kept = width // BS
    piece, wide = frames.shape
    vmem = pl.BlockSpec(memory_space=pltpu.VMEM)
    smem = pl.BlockSpec(memory_space=pltpu.SMEM)
    tall = 2 * rows + EXTRA
    pairs = pltpu.SemaphoreType.DMA((n,))
    small = (
        slope_blocks, prior_blocks, weight_ids[None], valid_mask[None],
        noise_weights[None], prior_weights[None], frames.T,
    )
    blocks, images = pl.pallas_call(
        functools.partial(exchange, n, noise_weights.shape[0]),
        out_shape=(
            jax.ShapeDtypeStruct((2, n, tall, width), jnp.bfloat16),
            jax.ShapeDtypeStruct((n, rows, 2 * wide), jnp.bfloat16),
        ),
        in_specs=[pl.BlockSpec(memory_space=pltpu.HBM)] * 9,
        out_specs=(vmem, vmem),
        scratch_shapes=[
            pltpu.VMEM((n, tall, width), jnp.bfloat16),
            pltpu.VMEM((piece, wide), jnp.bfloat16),
            pltpu.VMEM((n * piece, wide), jnp.bfloat16),
            pltpu.VMEM((n, rows, 2 * wide), jnp.bfloat16),
        ]
        + [pltpu.VMEM(x.shape, x.dtype) for x in small]
        + [
            pltpu.SemaphoreType.DMA((9,)),
            pairs, pairs, pairs, pairs, pairs, pairs, pairs,
            pltpu.SemaphoreType.DMA, pairs,
            pairs, pltpu.SemaphoreType.DMA,
            pairs, pairs, pairs, pairs,
        ],
        compiler_params=pltpu.CompilerParams(
            collective_id=0, has_side_effects=True, vmem_limit_bytes=32 * 1024 * 1024
        ),
    )(
        slope_matrix, prior_matrix, slope_blocks, prior_blocks, weight_ids[None], valid_mask[None],
        noise_weights[None], prior_weights[None], frames.T,
    )
    all_ids = blocks[:, :, 2 * rows, :2 * kept].astype(jnp.float32).astype(jnp.int32).reshape(-1)
    same = jnp.where(row == col, 0, 1).astype(jnp.int32)
    all_ids = jnp.concatenate([all_ids, same[None], col[None].astype(jnp.int32)])
    gram, applied = pl.pallas_call(
        functools.partial(combine, n),
        out_shape=(
            jax.ShapeDtypeStruct((AB * BS, AB * BS), jnp.float32),
            jax.ShapeDtypeStruct((wide, piece), jnp.float32),
        ),
        in_specs=[smem, vmem, vmem],
        out_specs=(vmem, vmem),
        scratch_shapes=[pltpu.VMEM((AB * BS, wide), jnp.float32)],
        compiler_params=pltpu.CompilerParams(vmem_limit_bytes=32 * 1024 * 1024),
    )(all_ids, blocks, images)
    return gram, applied.T


def solution(mesh):
    in_specs = (
        P(("groups", "row"), "col"),
        P(("groups", "row"), "col"),
        P(("groups", "row"), "col"),
        P(("groups", "row"), "col"),
        P(("groups", "row")),
        P(("groups", "row")),
        P("groups"),
        P(("groups", "row")),
        P(("groups", "row", "col"), None),
    )
    out_specs = (P(("groups", "row"), "col"), P(("groups", "row", "col"), None))
    return jax.shard_map(
        functools.partial(shards, mesh.shape["row"]),
        mesh=mesh, in_specs=in_specs, out_specs=out_specs, check_vma=False,
    )
```

```python
import functools

import jax
import jax.numpy as jnp
from jax import lax
from jax.experimental import pallas as pl
from jax.experimental.pallas import tpu as pltpu
from jax.sharding import PartitionSpec as P

BS = 128
AB = 6
EXTRA = 16
MESH = pl.DeviceIdType.MESH


def remote(src, dst, send, recv, axis, to):
    return pltpu.make_async_remote_copy(
        src_ref=src, dst_ref=dst, send_sem=send, recv_sem=recv,
        device_id={axis: to}, device_id_type=MESH,
    )


def exchange(
    n, classes, slope_hbm, prior_hbm, slope_ids_hbm, prior_ids_hbm,
    class_hbm, valid_hbm, noise_hbm, prior_weight_hbm, frames_hbm,
    blocks, images,
    held, own_frames, set_frames, partial,
    slope_ids, prior_ids, class_ids, valid, noise, prior_weight, frames_ref, load_sem,
    send_right, send_left, recv_z, send_c, recv_c, send_r, recv_r,
    send_p, recv_p, send_f, recv_f, send_v, recv_v, send_u, recv_u,
):
    row = lax.axis_index("row")
    col = lax.axis_index("col")
    rows, width = slope_hbm.shape
    kept = width // BS
    piece = own_frames.shape[0]
    loads = [
        pltpu.make_async_copy(src, dst, load_sem.at[k])
        for k, (src, dst) in enumerate(
            (
                (class_hbm, class_ids), (valid_hbm, valid), (noise_hbm, noise),
                (prior_weight_hbm, prior_weight), (slope_ids_hbm, slope_ids),
                (prior_ids_hbm, prior_ids), (frames_hbm, frames_ref),
                (slope_hbm, held.at[col, pl.ds(0, rows), :]),
                (prior_hbm, held.at[col, pl.ds(rows, rows), :]),
            )
        )
    ]
    for load in loads:
        load.start()
    barrier = pltpu.get_barrier_semaphore()
    for t in range(1, n):
        pl.semaphore_signal(barrier, inc=1, device_id={"col": lax.rem(col + t, n)}, device_id_type=MESH)
        pl.semaphore_signal(barrier, inc=1, device_id={"row": lax.rem(row + t, n)}, device_id_type=MESH)
    for load in loads:
        load.wait()
    own_frames[...] = jnp.transpose(frames_ref[...]).astype(jnp.bfloat16)
    subaps = class_ids.shape[1]
    picked = jnp.zeros((1, subaps), jnp.float32)
    for k in range(classes):
        picked = jnp.where(class_ids[...] == k, jnp.broadcast_to(noise[:, k:k + 1], picked.shape), picked)
    picked = (picked * valid[...].astype(jnp.float32)).astype(jnp.bfloat16)
    first = lax.broadcasted_iota(jnp.int32, (subaps, rows), 0) * (rows // subaps)
    lane = lax.broadcasted_iota(jnp.int32, (subaps, rows), 1)
    spread = (lane >= first) & (lane < first + rows // subaps)
    spread = jnp.where(spread, 1.0, 0.0).astype(jnp.bfloat16)
    slope_weight = jnp.dot(
        jnp.broadcast_to(picked, (EXTRA, subaps)), spread, preferred_element_type=jnp.float32
    )
    prior_wide = jnp.broadcast_to(prior_weight[...].astype(jnp.float32), (EXTRA, rows))
    weight = jnp.concatenate([slope_weight, prior_wide], axis=1)
    at_row = lax.broadcasted_iota(jnp.int32, (EXTRA, width), 0)
    at_lane = lax.broadcasted_iota(jnp.int32, (EXTRA, width), 1)
    names = jnp.zeros((EXTRA, width), jnp.int32)
    for part, ids in enumerate((slope_ids, prior_ids)):
        for k in range(kept):
            name = jnp.broadcast_to(ids[:, k:k + 1], names.shape) - col * AB
            names = jnp.where(at_lane == part * kept + k, name, names)
    extra = jnp.where(at_row == 0, names.astype(jnp.float32), weight)
    held[col, pl.ds(2 * rows, EXTRA), :] = extra.astype(jnp.bfloat16)
    pl.semaphore_wait(barrier, 2 * (n - 1))

    def frame_piece(source):
        return remote(
            own_frames, set_frames.at[pl.ds(source * piece, piece), :],
            send_p, recv_p.at[source], "col", row,
        )

    def right(t):
        source = col - t
        return remote(
            held.at[source], held.at[source], send_right.at[t], recv_z.at[source], "col", col + 1
        )

    def left(t):
        source = col + t
        return remote(
            held.at[source], held.at[source], send_left.at[t], recv_z.at[source], "col", col - 1
        )

    sibling = row + 1 - 2 * lax.rem(row, 2)

    def own_column(m):
        to = sibling if m == 0 else lax.rem(row + 2 * m, n)
        return remote(held.at[col], blocks.at[0, row], send_c.at[m], recv_c.at[row], "row", to)

    def pass_column(m):
        source = lax.rem(row + 2 * m, n)
        return remote(
            blocks.at[0, source], blocks.at[0, source], send_c.at[n // 2 + m], recv_c.at[source], "row", sibling
        )

    def came_column(source):
        return remote(blocks.at[0, source], blocks.at[0, source], send_c.at[0], recv_c.at[source], "row", sibling)

    def forward(source):
        return remote(
            held.at[source], blocks.at[1, row], send_r.at[source], recv_r.at[row], "row", source
        )

    def came_row(source):
        return remote(
            held.at[source], blocks.at[1, source], send_r.at[source], recv_r.at[source], "row", source
        )

    def whole_frames(s):
        return remote(
            set_frames, set_frames, send_f.at[s - 1], recv_f, "row", lax.rem(row + s, n)
        )

    @pl.when(row != col)
    def _():
        frame_piece(col).start()

    @pl.when(col < n - 1)
    def _():
        right(0).start()

    @pl.when(col > 0)
    def _():
        left(0).start()

    @pl.when(row == col)
    def _():
        set_frames[pl.ds(pl.multiple_of(col * piece, 16), piece), :] = own_frames[...]
        for t in range(1, n):
            frame_piece(lax.rem(col + t, n)).wait_recv()
        for s in range(1, n):
            whole_frames(s).start()

    for m in range(1, n // 2):
        own_column(m).start()
    own_column(0).start()
    blocks[0, row] = held[col]

    def use(source):
        @pl.when(source == row)
        def _():
            blocks[1, row] = held[row]

        @pl.when(source != row)
        def _():
            forward(source).start()

    def step(t):
        @pl.when(col - t >= 0)
        def _():
            came = right(t)
            came.wait_recv()

            @pl.when(col < n - 1)
            def _():
                came.start()

            use(col - t)

        @pl.when(col + t < n)
        def _():
            came = left(t)
            came.wait_recv()

            @pl.when(col > 0)
            def _():
                came.start()

            use(col + t)

        if t < n // 2:
            came_column(lax.rem(row + 2 * t, n)).wait_recv()
            pass_column(t).start()

    step(1)

    @pl.when(row != col)
    def _():
        whole_frames(1).wait_recv()

    parts = []
    for part, ids in enumerate((slope_ids, prior_ids)):
        total = jnp.zeros((rows, set_frames.shape[1]), jnp.float32)
        for k in range(kept):
            wanted = jnp.broadcast_to(ids[:, k:k + 1], (BS, set_frames.shape[1])) - col * AB
            chosen = jnp.zeros(wanted.shape, jnp.float32)
            for a in range(AB):
                block = set_frames[a * BS:(a + 1) * BS, :].astype(jnp.float32)
                chosen = jnp.where(wanted == a, block, chosen)
            total += jnp.dot(
                held[col, part * rows:(part + 1) * rows, k * BS:(k + 1) * BS], chosen.astype(jnp.bfloat16),
                preferred_element_type=jnp.float32,
            )
        parts.append(total)
    partial[col] = jnp.concatenate(parts, axis=1).astype(jnp.bfloat16)
    sends_v = []
    for t in range(1, n):
        copy = remote(
            partial.at[col], partial.at[col], send_v.at[t - 1], recv_v.at[t - 1], "col", lax.rem(col + t, n)
        )
        copy.start()
        sends_v.append(copy)

    for t in range(2, n):
        step(t)

    for copy in sends_v:
        copy.wait_recv()
    image = partial[0].astype(jnp.float32)
    for t in range(1, n):
        image += partial[t].astype(jnp.float32)
    images[row] = image.astype(jnp.bfloat16)
    sends_u = []
    for s in range(1, n):
        copy = remote(
            images.at[row], images.at[row], send_u.at[s - 1], recv_u.at[s - 1], "row", lax.rem(row + s, n)
        )
        copy.start()
        sends_u.append(copy)

    for m in range(n // 2):
        came_column(lax.rem(sibling + 2 * m, n)).wait_recv()

    @pl.when(row != col)
    def _():
        for s in range(1, n):
            came_row(lax.rem(row + s, n)).wait_recv()
        frame_piece(col).wait_send()

    @pl.when(row == col)
    def _():
        for s in range(1, n):
            whole_frames(s).wait_send()

    for copy in sends_u:
        copy.wait_recv()
    for t in range(1, n):
        source = lax.rem(col + t, n)

        @pl.when(source != row)
        def _():
            forward(source).wait_send()

    for t in range(n):
        @pl.when((col - t >= 0) & (col < n - 1))
        def _():
            right(t).wait_send()

        @pl.when((col + t < n) & (col > 0))
        def _():
            left(t).wait_send()

    for m in range(n // 2):
        own_column(m).wait_send()
        if m > 0:
            pass_column(m).wait_send()
    for copy in sends_v + sends_u:
        copy.wait_send()


def combine(n, ids_ref, blocks, images, gram, applied, total):
    rows = images.shape[1]
    kept = blocks.shape[3] // BS
    wide = images.shape[2] // 2
    same = ids_ref[4 * n * kept]
    quarter = ids_ref[4 * n * kept + 1]
    gram[...] = jnp.zeros_like(gram)
    total[...] = jnp.zeros_like(total)
    for i in range(n):
        for part in range(2):
            left = blocks[same, i, part * rows:(part + 1) * rows, :]
            right = blocks[0, i, part * rows:(part + 1) * rows, :].astype(jnp.float32)
            weight = blocks[0, i, 2 * rows:2 * rows + EXTRA, part * rows:(part + 1) * rows]
            weight = weight.astype(jnp.float32)[1:2, :]
            weight = jnp.transpose(jnp.broadcast_to(weight, (BS, rows)))
            right = jnp.concatenate(
                [right[:, k * BS:(k + 1) * BS] * weight for k in range(kept)], axis=1
            ).astype(jnp.bfloat16)
            image = images[i, :, part * wide:(part + 1) * wide].astype(jnp.float32)
            image = (image * weight[:, :wide]).astype(jnp.bfloat16)
            over = (((0,), (0,)), ((), ()))
            product = lax.dot_general(left, right, over, preferred_element_type=jnp.float32)
            shown = lax.dot_general(left, image, over, preferred_element_type=jnp.float32)
            for a in range(kept):
                down = ids_ref[(same * n + i) * 2 * kept + part * kept + a]
                down = pl.multiple_of(down * BS, BS)
                total[pl.ds(down, BS), :] += shown[a * BS:(a + 1) * BS]
                for b in range(kept):
                    across = ids_ref[i * 2 * kept + part * kept + b]
                    across = pl.multiple_of(across * BS, BS)
                    gram[pl.ds(down, BS), pl.ds(across, BS)] += product[
                        a * BS:(a + 1) * BS, b * BS:(b + 1) * BS
                    ]
    size = applied.shape[1]
    applied[...] = jnp.transpose(total[pl.ds(pl.multiple_of(quarter * size, 8), size), :])


def shards(
    n, slope_matrix, prior_matrix, slope_blocks, prior_blocks,
    weight_ids, valid_mask, noise_weights, prior_weights, frames,
):
    row = lax.axis_index("row")
    col = lax.axis_index("col")
    rows, width = slope_matrix.shape
    kept = width // BS
    piece, wide = frames.shape
    vmem = pl.BlockSpec(memory_space=pltpu.VMEM)
    smem = pl.BlockSpec(memory_space=pltpu.SMEM)
    tall = 2 * rows + EXTRA
    pairs = pltpu.SemaphoreType.DMA((n,))
    small = (
        slope_blocks, prior_blocks, weight_ids[None], valid_mask[None],
        noise_weights[None], prior_weights[None], frames.T,
    )
    blocks, images = pl.pallas_call(
        functools.partial(exchange, n, noise_weights.shape[0]),
        out_shape=(
            jax.ShapeDtypeStruct((2, n, tall, width), jnp.bfloat16),
            jax.ShapeDtypeStruct((n, rows, 2 * wide), jnp.bfloat16),
        ),
        in_specs=[pl.BlockSpec(memory_space=pltpu.HBM)] * 9,
        out_specs=(vmem, vmem),
        scratch_shapes=[
            pltpu.VMEM((n, tall, width), jnp.bfloat16),
            pltpu.VMEM((piece, wide), jnp.bfloat16),
            pltpu.VMEM((n * piece, wide), jnp.bfloat16),
            pltpu.VMEM((n, rows, 2 * wide), jnp.bfloat16),
        ]
        + [pltpu.VMEM(x.shape, x.dtype) for x in small]
        + [
            pltpu.SemaphoreType.DMA((9,)),
            pairs, pairs, pairs, pairs, pairs, pairs, pairs,
            pltpu.SemaphoreType.DMA, pairs,
            pairs, pltpu.SemaphoreType.DMA,
            pairs, pairs, pairs, pairs,
        ],
        compiler_params=pltpu.CompilerParams(
            collective_id=0, has_side_effects=True, vmem_limit_bytes=62 * 1024 * 1024
        ),
    )(
        slope_matrix, prior_matrix, slope_blocks, prior_blocks, weight_ids[None], valid_mask[None],
        noise_weights[None], prior_weights[None], frames.T,
    )
    all_ids = blocks[:, :, 2 * rows, :2 * kept].astype(jnp.float32).astype(jnp.int32).reshape(-1)
    same = jnp.where(row == col, 0, 1).astype(jnp.int32)
    all_ids = jnp.concatenate([all_ids, same[None], col[None].astype(jnp.int32)])
    gram, applied = pl.pallas_call(
        functools.partial(combine, n),
        out_shape=(
            jax.ShapeDtypeStruct((AB * BS, AB * BS), jnp.float32),
            jax.ShapeDtypeStruct((wide, piece), jnp.float32),
        ),
        in_specs=[smem, vmem, vmem],
        out_specs=(vmem, vmem),
        scratch_shapes=[pltpu.VMEM((AB * BS, wide), jnp.float32)],
        compiler_params=pltpu.CompilerParams(vmem_limit_bytes=32 * 1024 * 1024),
    )(all_ids, blocks, images)
    return gram, applied.T


def solution(mesh):
    in_specs = (
        P(("groups", "row"), "col"),
        P(("groups", "row"), "col"),
        P(("groups", "row"), "col"),
        P(("groups", "row"), "col"),
        P(("groups", "row")),
        P(("groups", "row")),
        P("groups"),
        P(("groups", "row")),
        P(("groups", "row", "col"), None),
    )
    out_specs = (P(("groups", "row"), "col"), P(("groups", "row", "col"), None))
    return jax.shard_map(
        functools.partial(shards, mesh.shape["row"]),
        mesh=mesh, in_specs=in_specs, out_specs=out_specs, check_vma=False,
    )
```

```python
import functools

import jax
import jax.numpy as jnp
from jax import lax
from jax.experimental import pallas as pl
from jax.experimental.pallas import tpu as pltpu
from jax.sharding import PartitionSpec as P

BS = 128
AB = 6
EXTRA = 16
MESH = pl.DeviceIdType.MESH


def remote(src, dst, send, recv, axis, to):
    return pltpu.make_async_remote_copy(
        src_ref=src, dst_ref=dst, send_sem=send, recv_sem=recv,
        device_id={axis: to}, device_id_type=MESH,
    )


def exchange(
    n, classes, slope_hbm, prior_hbm, slope_ids_hbm, prior_ids_hbm,
    class_hbm, valid_hbm, noise_hbm, prior_weight_hbm, frames_hbm,
    blocks, images,
    held, own_frames, set_frames, flat_frames, partial,
    slope_ids, prior_ids, class_ids, valid, noise, prior_weight, frames_ref, load_sem,
    send_right, send_left, recv_z, send_c, recv_c, send_r, recv_r,
    send_p, recv_p, send_f, recv_f, send_v, recv_v, send_u, recv_u,
):
    row = lax.axis_index("row")
    col = lax.axis_index("col")
    rows, width = slope_hbm.shape
    kept = width // BS
    piece = own_frames.shape[0]
    loads = [
        pltpu.make_async_copy(src, dst, load_sem.at[k])
        for k, (src, dst) in enumerate(
            (
                (class_hbm, class_ids), (valid_hbm, valid), (noise_hbm, noise),
                (prior_weight_hbm, prior_weight), (slope_ids_hbm, slope_ids),
                (prior_ids_hbm, prior_ids), (frames_hbm, frames_ref),
                (slope_hbm, held.at[col, pl.ds(0, rows), :]),
                (prior_hbm, held.at[col, pl.ds(rows, rows), :]),
            )
        )
    ]
    for load in loads:
        load.start()
    barrier = pltpu.get_barrier_semaphore()
    for t in range(1, n):
        pl.semaphore_signal(barrier, inc=1, device_id={"col": lax.rem(col + t, n)}, device_id_type=MESH)
        pl.semaphore_signal(barrier, inc=1, device_id={"row": lax.rem(row + t, n)}, device_id_type=MESH)
    for load in loads:
        load.wait()
    turned = jnp.transpose(frames_ref[...])
    pack = turned.shape[0] // piece
    own_frames[...] = jnp.concatenate(
        [turned[h * piece:(h + 1) * piece] for h in range(pack)], axis=1
    ).astype(jnp.bfloat16)
    subaps = class_ids.shape[1]
    picked = jnp.zeros((1, subaps), jnp.float32)
    for k in range(classes):
        picked = jnp.where(class_ids[...] == k, jnp.broadcast_to(noise[:, k:k + 1], picked.shape), picked)
    picked = (picked * valid[...].astype(jnp.float32)).astype(jnp.bfloat16)
    first = lax.broadcasted_iota(jnp.int32, (subaps, rows), 0) * (rows // subaps)
    lane = lax.broadcasted_iota(jnp.int32, (subaps, rows), 1)
    spread = (lane >= first) & (lane < first + rows // subaps)
    spread = jnp.where(spread, 1.0, 0.0).astype(jnp.bfloat16)
    slope_weight = jnp.dot(
        jnp.broadcast_to(picked, (EXTRA, subaps)), spread, preferred_element_type=jnp.float32
    )
    prior_wide = jnp.broadcast_to(prior_weight[...].astype(jnp.float32), (EXTRA, rows))
    weight = jnp.concatenate([slope_weight, prior_wide], axis=1)
    at_row = lax.broadcasted_iota(jnp.int32, (EXTRA, width), 0)
    at_lane = lax.broadcasted_iota(jnp.int32, (EXTRA, width), 1)
    names = jnp.zeros((EXTRA, width), jnp.int32)
    for part, ids in enumerate((slope_ids, prior_ids)):
        for k in range(kept):
            name = jnp.broadcast_to(ids[:, k:k + 1], names.shape) - col * AB
            names = jnp.where(at_lane == part * kept + k, name, names)
    extra = jnp.where(at_row == 0, names.astype(jnp.float32), weight)
    held[col, pl.ds(2 * rows, EXTRA), :] = extra.astype(jnp.bfloat16)
    pl.semaphore_wait(barrier, 2 * (n - 1))

    def frame_piece(source):
        return remote(
            own_frames, set_frames.at[pl.ds(source * piece, piece), :],
            send_p, recv_p.at[source], "col", row,
        )

    def right(t):
        source = col - t
        return remote(
            held.at[source], held.at[source], send_right.at[t], recv_z.at[source], "col", col + 1
        )

    def left(t):
        source = col + t
        return remote(
            held.at[source], held.at[source], send_left.at[t], recv_z.at[source], "col", col - 1
        )

    sibling = row + 1 - 2 * lax.rem(row, 2)

    def own_column(m):
        to = sibling if m == 0 else lax.rem(row + 2 * m, n)
        return remote(held.at[col], blocks.at[0, row], send_c.at[m], recv_c.at[row], "row", to)

    def pass_column(m):
        source = lax.rem(row + 2 * m, n)
        return remote(
            blocks.at[0, source], blocks.at[0, source], send_c.at[n // 2 + m], recv_c.at[source], "row", sibling
        )

    def came_column(source):
        return remote(blocks.at[0, source], blocks.at[0, source], send_c.at[0], recv_c.at[source], "row", sibling)

    def forward(source):
        return remote(
            held.at[source], blocks.at[1, row], send_r.at[source], recv_r.at[row], "row", source
        )

    def came_row(source):
        return remote(
            held.at[source], blocks.at[1, source], send_r.at[source], recv_r.at[source], "row", source
        )

    def whole_frames(s):
        return remote(
            set_frames, set_frames, send_f.at[s - 1], recv_f, "row", lax.rem(row + s, n)
        )

    @pl.when(row != col)
    def _():
        frame_piece(col).start()

    @pl.when(col < n - 1)
    def _():
        right(0).start()

    @pl.when(col > 0)
    def _():
        left(0).start()

    @pl.when(row == col)
    def _():
        set_frames[pl.ds(pl.multiple_of(col * piece, 16), piece), :] = own_frames[...]
        for t in range(1, n):
            frame_piece(lax.rem(col + t, n)).wait_recv()
        for s in range(1, n):
            whole_frames(s).start()

    for m in range(1, n // 2):
        own_column(m).start()
    own_column(0).start()
    blocks[0, row] = held[col]

    def use(source):
        @pl.when(source == row)
        def _():
            blocks[1, row] = held[row]

        @pl.when(source != row)
        def _():
            forward(source).start()

    def step(t):
        @pl.when(col - t >= 0)
        def _():
            came = right(t)
            came.wait_recv()

            @pl.when(col < n - 1)
            def _():
                came.start()

            use(col - t)

        @pl.when(col + t < n)
        def _():
            came = left(t)
            came.wait_recv()

            @pl.when(col > 0)
            def _():
                came.start()

            use(col + t)

        if t < n // 2:
            came_column(lax.rem(row + 2 * t, n)).wait_recv()
            pass_column(t).start()

    step(1)

    @pl.when(row != col)
    def _():
        whole_frames(1).wait_recv()

    wide = turned.shape[1]
    for k in range(n):
        for h in range(pack):
            flat_frames[pl.ds((k * pack + h) * piece, piece), :] = set_frames[
                k * piece:(k + 1) * piece, h * wide:(h + 1) * wide
            ]
    parts = []
    for part, ids in enumerate((slope_ids, prior_ids)):
        total = jnp.zeros((rows, wide), jnp.float32)
        for k in range(kept):
            wanted = jnp.broadcast_to(ids[:, k:k + 1], (BS, wide)) - col * AB
            chosen = jnp.zeros(wanted.shape, jnp.float32)
            for a in range(AB):
                block = flat_frames[a * BS:(a + 1) * BS, :].astype(jnp.float32)
                chosen = jnp.where(wanted == a, block, chosen)
            total += jnp.dot(
                held[col, part * rows:(part + 1) * rows, k * BS:(k + 1) * BS], chosen.astype(jnp.bfloat16),
                preferred_element_type=jnp.float32,
            )
        parts.append(total)
    partial[col] = jnp.concatenate(parts, axis=1).astype(jnp.bfloat16)
    sends_v = []
    for t in range(1, n):
        copy = remote(
            partial.at[col], partial.at[col], send_v.at[t - 1], recv_v.at[t - 1], "col", lax.rem(col + t, n)
        )
        copy.start()
        sends_v.append(copy)

    for t in range(2, n - 1):
        step(t)

    for copy in sends_v:
        copy.wait_recv()
    image = partial[0].astype(jnp.float32)
    for t in range(1, n):
        image += partial[t].astype(jnp.float32)
    images[row] = image.astype(jnp.bfloat16)
    sends_u = []
    for s in range(1, n):
        copy = remote(
            images.at[row], images.at[row], send_u.at[s - 1], recv_u.at[s - 1], "row", lax.rem(row + s, n)
        )
        copy.start()
        sends_u.append(copy)

    step(n - 1)

    for m in range(n // 2):
        came_column(lax.rem(sibling + 2 * m, n)).wait_recv()

    @pl.when(row != col)
    def _():
        for s in range(1, n):
            came_row(lax.rem(row + s, n)).wait_recv()
        frame_piece(col).wait_send()

    @pl.when(row == col)
    def _():
        for s in range(1, n):
            whole_frames(s).wait_send()

    for copy in sends_u:
        copy.wait_recv()
    for t in range(1, n):
        source = lax.rem(col + t, n)

        @pl.when(source != row)
        def _():
            forward(source).wait_send()

    for t in range(n):
        @pl.when((col - t >= 0) & (col < n - 1))
        def _():
            right(t).wait_send()

        @pl.when((col + t < n) & (col > 0))
        def _():
            left(t).wait_send()

    for m in range(n // 2):
        own_column(m).wait_send()
        if m > 0:
            pass_column(m).wait_send()
    for copy in sends_v + sends_u:
        copy.wait_send()


def combine(n, ids_ref, blocks, images, gram, applied, total):
    rows = images.shape[1]
    kept = blocks.shape[3] // BS
    wide = images.shape[2] // 2
    same = ids_ref[4 * n * kept]
    quarter = ids_ref[4 * n * kept + 1]
    gram[...] = jnp.zeros_like(gram)
    total[...] = jnp.zeros_like(total)
    for i in range(n):
        for part in range(2):
            left = blocks[same, i, part * rows:(part + 1) * rows, :]
            right = blocks[0, i, part * rows:(part + 1) * rows, :].astype(jnp.float32)
            weight = blocks[0, i, 2 * rows:2 * rows + EXTRA, part * rows:(part + 1) * rows]
            weight = weight.astype(jnp.float32)[1:2, :]
            weight = jnp.transpose(jnp.broadcast_to(weight, (BS, rows)))
            right = jnp.concatenate(
                [right[:, k * BS:(k + 1) * BS] * weight for k in range(kept)], axis=1
            ).astype(jnp.bfloat16)
            image = images[i, :, part * wide:(part + 1) * wide].astype(jnp.float32)
            image = (image * weight[:, :wide]).astype(jnp.bfloat16)
            over = (((0,), (0,)), ((), ()))
            product = lax.dot_general(left, right, over, preferred_element_type=jnp.float32)
            shown = lax.dot_general(left, image, over, preferred_element_type=jnp.float32)
            for a in range(kept):
                down = ids_ref[(same * n + i) * 2 * kept + part * kept + a]
                down = pl.multiple_of(down * BS, BS)
                total[pl.ds(down, BS), :] += shown[a * BS:(a + 1) * BS]
                for b in range(kept):
                    across = ids_ref[i * 2 * kept + part * kept + b]
                    across = pl.multiple_of(across * BS, BS)
                    gram[pl.ds(down, BS), pl.ds(across, BS)] += product[
                        a * BS:(a + 1) * BS, b * BS:(b + 1) * BS
                    ]
    size = applied.shape[1]
    applied[...] = jnp.transpose(total[pl.ds(pl.multiple_of(quarter * size, 8), size), :])


def shards(
    n, slope_matrix, prior_matrix, slope_blocks, prior_blocks,
    weight_ids, valid_mask, noise_weights, prior_weights, frames,
):
    row = lax.axis_index("row")
    col = lax.axis_index("col")
    rows, width = slope_matrix.shape
    kept = width // BS
    piece, wide = frames.shape
    vmem = pl.BlockSpec(memory_space=pltpu.VMEM)
    smem = pl.BlockSpec(memory_space=pltpu.SMEM)
    tall = 2 * rows + EXTRA
    pack = 2 if piece % 32 == 0 else 1
    pairs = pltpu.SemaphoreType.DMA((n,))
    small = (
        slope_blocks, prior_blocks, weight_ids[None], valid_mask[None],
        noise_weights[None], prior_weights[None], frames.T,
    )
    blocks, images = pl.pallas_call(
        functools.partial(exchange, n, noise_weights.shape[0]),
        out_shape=(
            jax.ShapeDtypeStruct((2, n, tall, width), jnp.bfloat16),
            jax.ShapeDtypeStruct((n, rows, 2 * wide), jnp.bfloat16),
        ),
        in_specs=[pl.BlockSpec(memory_space=pltpu.HBM)] * 9,
        out_specs=(vmem, vmem),
        scratch_shapes=[
            pltpu.VMEM((n, tall, width), jnp.bfloat16),
            pltpu.VMEM((piece // pack, wide * pack), jnp.bfloat16),
            pltpu.VMEM((n * piece // pack, wide * pack), jnp.bfloat16),
            pltpu.VMEM((n * piece, wide), jnp.bfloat16),
            pltpu.VMEM((n, rows, 2 * wide), jnp.bfloat16),
        ]
        + [pltpu.VMEM(x.shape, x.dtype) for x in small]
        + [
            pltpu.SemaphoreType.DMA((9,)),
            pairs, pairs, pairs, pairs, pairs, pairs, pairs,
            pltpu.SemaphoreType.DMA, pairs,
            pairs, pltpu.SemaphoreType.DMA,
            pairs, pairs, pairs, pairs,
        ],
        compiler_params=pltpu.CompilerParams(
            collective_id=0, has_side_effects=True, vmem_limit_bytes=62 * 1024 * 1024
        ),
    )(
        slope_matrix, prior_matrix, slope_blocks, prior_blocks, weight_ids[None], valid_mask[None],
        noise_weights[None], prior_weights[None], frames.T,
    )
    all_ids = blocks[:, :, 2 * rows, :2 * kept].astype(jnp.float32).astype(jnp.int32).reshape(-1)
    same = jnp.where(row == col, 0, 1).astype(jnp.int32)
    all_ids = jnp.concatenate([all_ids, same[None], col[None].astype(jnp.int32)])
    gram, applied = pl.pallas_call(
        functools.partial(combine, n),
        out_shape=(
            jax.ShapeDtypeStruct((AB * BS, AB * BS), jnp.float32),
            jax.ShapeDtypeStruct((wide, piece), jnp.float32),
        ),
        in_specs=[smem, vmem, vmem],
        out_specs=(vmem, vmem),
        scratch_shapes=[pltpu.VMEM((AB * BS, wide), jnp.float32)],
        compiler_params=pltpu.CompilerParams(vmem_limit_bytes=62 * 1024 * 1024),
    )(all_ids, blocks, images)
    return gram, applied.T


def solution(mesh):
    in_specs = (
        P(("groups", "row"), "col"),
        P(("groups", "row"), "col"),
        P(("groups", "row"), "col"),
        P(("groups", "row"), "col"),
        P(("groups", "row")),
        P(("groups", "row")),
        P("groups"),
        P(("groups", "row")),
        P(("groups", "row", "col"), None),
    )
    out_specs = (P(("groups", "row"), "col"), P(("groups", "row", "col"), None))
    return jax.shard_map(
        functools.partial(shards, mesh.shape["row"]),
        mesh=mesh, in_specs=in_specs, out_specs=out_specs, check_vma=False,
    )
```

```python
import functools

import jax
import jax.numpy as jnp
from jax import lax
from jax.experimental import pallas as pl
from jax.experimental.pallas import tpu as pltpu
from jax.sharding import PartitionSpec as P

BS = 128
AB = 6
EXTRA = 16
MESH = pl.DeviceIdType.MESH


def remote(src, dst, send, recv, axis, to):
    return pltpu.make_async_remote_copy(
        src_ref=src, dst_ref=dst, send_sem=send, recv_sem=recv,
        device_id={axis: to}, device_id_type=MESH,
    )


def exchange(
    n, classes, slope_hbm, prior_hbm, slope_ids_hbm, prior_ids_hbm,
    class_hbm, valid_hbm, noise_hbm, prior_weight_hbm, frames_hbm,
    blocks, images,
    held, own_frames, set_frames, flat_frames, partial,
    slope_ids, prior_ids, class_ids, valid, noise, prior_weight, frames_ref, load_sem,
    send_right, send_left, recv_z, send_c, recv_c, send_r, recv_r,
    send_p, recv_p, send_f, recv_f, send_v, recv_v, send_u, recv_u,
):
    row = lax.axis_index("row")
    col = lax.axis_index("col")
    rows, width = slope_hbm.shape
    kept = width // BS
    piece = own_frames.shape[0]
    loads = [
        pltpu.make_async_copy(src, dst, load_sem.at[k])
        for k, (src, dst) in enumerate(
            (
                (class_hbm, class_ids), (valid_hbm, valid), (noise_hbm, noise),
                (prior_weight_hbm, prior_weight), (slope_ids_hbm, slope_ids),
                (prior_ids_hbm, prior_ids), (frames_hbm, frames_ref),
                (slope_hbm, held.at[col, pl.ds(0, rows), :]),
                (prior_hbm, held.at[col, pl.ds(rows, rows), :]),
            )
        )
    ]
    for load in loads:
        load.start()
    barrier = pltpu.get_barrier_semaphore()
    for t in range(1, n):
        pl.semaphore_signal(barrier, inc=1, device_id={"col": lax.rem(col + t, n)}, device_id_type=MESH)
        pl.semaphore_signal(barrier, inc=1, device_id={"row": lax.rem(row + t, n)}, device_id_type=MESH)
    for load in loads:
        load.wait()
    turned = jnp.transpose(frames_ref[...])
    pack = turned.shape[0] // piece
    own_frames[...] = jnp.concatenate(
        [turned[h * piece:(h + 1) * piece] for h in range(pack)], axis=1
    ).astype(jnp.bfloat16)
    subaps = class_ids.shape[1]
    picked = jnp.zeros((1, subaps), jnp.float32)
    for k in range(classes):
        picked = jnp.where(class_ids[...] == k, jnp.broadcast_to(noise[:, k:k + 1], picked.shape), picked)
    picked = (picked * valid[...].astype(jnp.float32)).astype(jnp.bfloat16)
    first = lax.broadcasted_iota(jnp.int32, (subaps, rows), 0) * (rows // subaps)
    lane = lax.broadcasted_iota(jnp.int32, (subaps, rows), 1)
    spread = (lane >= first) & (lane < first + rows // subaps)
    spread = jnp.where(spread, 1.0, 0.0).astype(jnp.bfloat16)
    slope_weight = jnp.dot(
        jnp.broadcast_to(picked, (EXTRA, subaps)), spread, preferred_element_type=jnp.float32
    )
    prior_wide = jnp.broadcast_to(prior_weight[...].astype(jnp.float32), (EXTRA, rows))
    weight = jnp.concatenate([slope_weight, prior_wide], axis=1)
    at_row = lax.broadcasted_iota(jnp.int32, (EXTRA, width), 0)
    at_lane = lax.broadcasted_iota(jnp.int32, (EXTRA, width), 1)
    names = jnp.zeros((EXTRA, width), jnp.int32)
    for part, ids in enumerate((slope_ids, prior_ids)):
        for k in range(kept):
            name = jnp.broadcast_to(ids[:, k:k + 1], names.shape) - col * AB
            names = jnp.where(at_lane == part * kept + k, name, names)
    extra = jnp.where(at_row == 0, names.astype(jnp.float32), weight)
    held[col, pl.ds(2 * rows, EXTRA), :] = extra.astype(jnp.bfloat16)
    pl.semaphore_wait(barrier, 2 * (n - 1))

    def frame_piece(source):
        return remote(
            own_frames, set_frames.at[pl.ds(source * piece, piece), :],
            send_p, recv_p.at[source], "col", row,
        )

    def right(t):
        source = col - t
        return remote(
            held.at[source], held.at[source], send_right.at[t], recv_z.at[source], "col", col + 1
        )

    def left(t):
        source = col + t
        return remote(
            held.at[source], held.at[source], send_left.at[t], recv_z.at[source], "col", col - 1
        )

    sibling = row + 1 - 2 * lax.rem(row, 2)

    def own_column(m):
        to = sibling if m == 0 else lax.rem(row + 2 * m, n)
        return remote(held.at[col], blocks.at[0, row], send_c.at[m], recv_c.at[row], "row", to)

    def pass_column(m):
        source = lax.rem(row + 2 * m, n)
        return remote(
            blocks.at[0, source], blocks.at[0, source], send_c.at[n // 2 + m], recv_c.at[source], "row", sibling
        )

    def came_column(source):
        return remote(blocks.at[0, source], blocks.at[0, source], send_c.at[0], recv_c.at[source], "row", sibling)

    def forward(source):
        return remote(
            held.at[source], blocks.at[1, row], send_r.at[source], recv_r.at[row], "row", source
        )

    def came_row(source):
        return remote(
            held.at[source], blocks.at[1, source], send_r.at[source], recv_r.at[source], "row", source
        )

    def whole_frames(s):
        return remote(
            set_frames, set_frames, send_f.at[s - 1], recv_f, "row", lax.rem(row + s, n)
        )

    @pl.when(row != col)
    def _():
        frame_piece(col).start()

    @pl.when(col < n - 1)
    def _():
        right(0).start()

    @pl.when(col > 0)
    def _():
        left(0).start()

    @pl.when(row == col)
    def _():
        set_frames[pl.ds(pl.multiple_of(col * piece, 16), piece), :] = own_frames[...]
        for t in range(1, n):
            frame_piece(lax.rem(col + t, n)).wait_recv()
        for s in range(1, n):
            whole_frames(s).start()

    for m in range(1, n // 2):
        own_column(m).start()
    own_column(0).start()
    blocks[0, row] = held[col]

    def use(source):
        @pl.when(source == row)
        def _():
            blocks[1, row] = held[row]

        @pl.when(source != row)
        def _():
            forward(source).start()

    def step(t):
        @pl.when(col - t >= 0)
        def _():
            came = right(t)
            came.wait_recv()

            @pl.when(col < n - 1)
            def _():
                came.start()

            use(col - t)

        @pl.when(col + t < n)
        def _():
            came = left(t)
            came.wait_recv()

            @pl.when(col > 0)
            def _():
                came.start()

            use(col + t)

    step(1)

    @pl.when(row != col)
    def _():
        whole_frames(1).wait_recv()

    wide = turned.shape[1]
    for k in range(n):
        for h in range(pack):
            flat_frames[pl.ds((k * pack + h) * piece, piece), :] = set_frames[
                k * piece:(k + 1) * piece, h * wide:(h + 1) * wide
            ]
    parts = []
    for part, ids in enumerate((slope_ids, prior_ids)):
        total = jnp.zeros((rows, wide), jnp.float32)
        for k in range(kept):
            wanted = jnp.broadcast_to(ids[:, k:k + 1], (BS, wide)) - col * AB
            chosen = jnp.zeros(wanted.shape, jnp.float32)
            for a in range(AB):
                block = flat_frames[a * BS:(a + 1) * BS, :].astype(jnp.float32)
                chosen = jnp.where(wanted == a, block, chosen)
            total += jnp.dot(
                held[col, part * rows:(part + 1) * rows, k * BS:(k + 1) * BS], chosen.astype(jnp.bfloat16),
                preferred_element_type=jnp.float32,
            )
        parts.append(total)
    partial[col] = jnp.concatenate(parts, axis=1).astype(jnp.bfloat16)
    sends_v = []
    for t in range(1, n):
        copy = remote(
            partial.at[col], partial.at[col], send_v.at[t - 1], recv_v.at[t - 1], "col", lax.rem(col + t, n)
        )
        copy.start()
        sends_v.append(copy)

    for t in range(2, n - 1):
        step(t)
    for m in range(1, n // 2):
        came_column(lax.rem(row + 2 * m, n)).wait_recv()
        pass_column(m).start()

    for copy in sends_v:
        copy.wait_recv()
    image = partial[0].astype(jnp.float32)
    for t in range(1, n):
        image += partial[t].astype(jnp.float32)
    images[row] = image.astype(jnp.bfloat16)
    sends_u = []
    for s in range(1, n):
        copy = remote(
            images.at[row], images.at[row], send_u.at[s - 1], recv_u.at[s - 1], "row", lax.rem(row + s, n)
        )
        copy.start()
        sends_u.append(copy)

    step(n - 1)

    for m in range(n // 2):
        came_column(lax.rem(sibling + 2 * m, n)).wait_recv()

    @pl.when(row != col)
    def _():
        for s in range(1, n):
            came_row(lax.rem(row + s, n)).wait_recv()
        frame_piece(col).wait_send()

    @pl.when(row == col)
    def _():
        for s in range(1, n):
            whole_frames(s).wait_send()

    for copy in sends_u:
        copy.wait_recv()
    for t in range(1, n):
        source = lax.rem(col + t, n)

        @pl.when(source != row)
        def _():
            forward(source).wait_send()

    for t in range(n):
        @pl.when((col - t >= 0) & (col < n - 1))
        def _():
            right(t).wait_send()

        @pl.when((col + t < n) & (col > 0))
        def _():
            left(t).wait_send()

    for m in range(n // 2):
        own_column(m).wait_send()
        if m > 0:
            pass_column(m).wait_send()
    for copy in sends_v + sends_u:
        copy.wait_send()


def combine(n, blocks, images, gram, applied, total, ids_wide, ids_ref, ids_sem):
    rows = images.shape[1]
    kept = blocks.shape[3] // BS
    wide = images.shape[2] // 2
    quarter = lax.axis_index("col")
    same = jnp.where(lax.axis_index("row") == quarter, 0, 1)
    for slot in range(2):
        for i in range(n):
            names = blocks[slot, i, 2 * rows:2 * rows + EXTRA, 0:BS].astype(jnp.float32)
            ids_wide[slot * n + i:slot * n + i + 1, :] = names[0:1, :].astype(jnp.int32)
    copy = pltpu.make_async_copy(ids_wide, ids_ref, ids_sem)
    copy.start()
    gram[...] = jnp.zeros_like(gram)
    total[...] = jnp.zeros_like(total)
    copy.wait()
    for i in range(n):
        for part in range(2):
            left = blocks[same, i, part * rows:(part + 1) * rows, :]
            right = blocks[0, i, part * rows:(part + 1) * rows, :].astype(jnp.float32)
            weight = blocks[0, i, 2 * rows:2 * rows + EXTRA, part * rows:(part + 1) * rows]
            weight = weight.astype(jnp.float32)[1:2, :]
            weight = jnp.transpose(jnp.broadcast_to(weight, (BS, rows)))
            right = jnp.concatenate(
                [right[:, k * BS:(k + 1) * BS] * weight for k in range(kept)], axis=1
            ).astype(jnp.bfloat16)
            image = images[i, :, part * wide:(part + 1) * wide].astype(jnp.float32)
            image = (image * weight[:, :wide]).astype(jnp.bfloat16)
            over = (((0,), (0,)), ((), ()))
            product = lax.dot_general(left, right, over, preferred_element_type=jnp.float32)
            shown = lax.dot_general(left, image, over, preferred_element_type=jnp.float32)
            for a in range(kept):
                down = ids_ref[same * n + i, part * kept + a]
                down = pl.multiple_of(down * BS, BS)
                total[pl.ds(down, BS), :] += shown[a * BS:(a + 1) * BS]
                for b in range(kept):
                    across = ids_ref[i, part * kept + b]
                    across = pl.multiple_of(across * BS, BS)
                    gram[pl.ds(down, BS), pl.ds(across, BS)] += product[
                        a * BS:(a + 1) * BS, b * BS:(b + 1) * BS
                    ]
    size = applied.shape[1]
    applied[...] = jnp.transpose(total[pl.ds(pl.multiple_of(quarter * size, 8), size), :])


def shards(
    n, slope_matrix, prior_matrix, slope_blocks, prior_blocks,
    weight_ids, valid_mask, noise_weights, prior_weights, frames,
):
    rows, width = slope_matrix.shape
    kept = width // BS
    piece, wide = frames.shape
    vmem = pl.BlockSpec(memory_space=pltpu.VMEM)
    tall = 2 * rows + EXTRA
    pack = 2 if piece % 32 == 0 else 1
    pairs = pltpu.SemaphoreType.DMA((n,))
    small = (
        slope_blocks, prior_blocks, weight_ids[None], valid_mask[None],
        noise_weights[None], prior_weights[None], frames.T,
    )
    blocks, images = pl.pallas_call(
        functools.partial(exchange, n, noise_weights.shape[0]),
        out_shape=(
            jax.ShapeDtypeStruct((2, n, tall, width), jnp.bfloat16),
            jax.ShapeDtypeStruct((n, rows, 2 * wide), jnp.bfloat16),
        ),
        in_specs=[pl.BlockSpec(memory_space=pltpu.HBM)] * 9,
        out_specs=(vmem, vmem),
        scratch_shapes=[
            pltpu.VMEM((n, tall, width), jnp.bfloat16),
            pltpu.VMEM((piece // pack, wide * pack), jnp.bfloat16),
            pltpu.VMEM((n * piece // pack, wide * pack), jnp.bfloat16),
            pltpu.VMEM((n * piece, wide), jnp.bfloat16),
            pltpu.VMEM((n, rows, 2 * wide), jnp.bfloat16),
        ]
        + [pltpu.VMEM(x.shape, x.dtype) for x in small]
        + [
            pltpu.SemaphoreType.DMA((9,)),
            pairs, pairs, pairs, pairs, pairs, pairs, pairs,
            pltpu.SemaphoreType.DMA, pairs,
            pairs, pltpu.SemaphoreType.DMA,
            pairs, pairs, pairs, pairs,
        ],
        compiler_params=pltpu.CompilerParams(
            collective_id=0, has_side_effects=True, vmem_limit_bytes=62 * 1024 * 1024
        ),
    )(
        slope_matrix, prior_matrix, slope_blocks, prior_blocks, weight_ids[None], valid_mask[None],
        noise_weights[None], prior_weights[None], frames.T,
    )
    gram, applied = pl.pallas_call(
        functools.partial(combine, n),
        out_shape=(
            jax.ShapeDtypeStruct((AB * BS, AB * BS), jnp.float32),
            jax.ShapeDtypeStruct((wide, piece), jnp.float32),
        ),
        in_specs=[vmem, vmem],
        out_specs=(vmem, vmem),
        scratch_shapes=[
            pltpu.VMEM((AB * BS, wide), jnp.float32),
            pltpu.VMEM((2 * n, BS), jnp.int32),
            pltpu.SMEM((2 * n, BS), jnp.int32),
            pltpu.SemaphoreType.DMA,
        ],
        compiler_params=pltpu.CompilerParams(vmem_limit_bytes=62 * 1024 * 1024),
    )(blocks, images)
    return gram, applied.T


def solution(mesh):
    in_specs = (
        P(("groups", "row"), "col"),
        P(("groups", "row"), "col"),
        P(("groups", "row"), "col"),
        P(("groups", "row"), "col"),
        P(("groups", "row")),
        P(("groups", "row")),
        P("groups"),
        P(("groups", "row")),
        P(("groups", "row", "col"), None),
    )
    out_specs = (P(("groups", "row"), "col"), P(("groups", "row", "col"), None))
    return jax.shard_map(
        functools.partial(shards, mesh.shape["row"]),
        mesh=mesh, in_specs=in_specs, out_specs=out_specs, check_vma=False,
    )
```
